32 devices in a mesh: lat: 8 (over y, x, core), lon: 4 (over z).
Axes of the slice: x: 2, y: 2, z: 4, core: 2. Of those that a mesh axis runs over, the one named last changes fastest.
Arguments:
- queries: bfloat16 [128, 64, 1024], P('lat', 'lon'), may hold values from -80 to 80
- keys: bfloat16 [128, 64, 1024], P('lat', 'lon'), may hold values from -6 to 6
- values: bfloat16 [128, 64, 1024], P('lat', 'lon'), may hold values from -6 to 6
- grad_out: bfloat16 [128, 64, 1024], P('lat', 'lon'), may hold values from -6 to 6
- fold_cols: int32 [2, 64], replicated, may hold values from 0 to 63, as said below
Outputs:
- grad_queries: bfloat16 [128, 64, 1024], P('lat', 'lon')
- grad_keys: bfloat16 [128, 64, 1024], P('lat', 'lon')
- grad_values: bfloat16 [128, 64, 1024], P('lat', 'lon')
The draws below stay inside these ranges and needn't reach their ends.
Inputs may be any that keep to these rules, and one draw needn't show every extreme that they name: Each row of fold_cols maps, for every block b of 16 columns, the runs [b * 16, b * 16 + 4), [b * 16 + 4, (b + 1) * 16 - 4) and [(b + 1) * 16 - 4, (b + 1) * 16) one to one onto the same runs of the block 2 blocks further on the loop.
All inputs are finite; a program needn't handle non-finite values.
Results may differ from the reference program's by a relative error of at most 0.0075.
Values may be sent and summed in bfloat16 or wider, within the bound.
A program may use at most 128 MiB of HBM per device.

```python
import jax
import jax.numpy as jnp
from jax import lax

HEADS = 16
HEAD_DIM = 64
WIDTH = 1024
RADIUS = 4
TW = 16
NLAT = 128
NLON = 64


def query_key_pair(key):
    grid_shape = (NLAT, NLON, WIDTH)
    base_keys = jax.random.truncated_normal(jax.random.fold_in(key, 101), -6.0, 6.0, grid_shape, jnp.float32)
    base_queries = jax.random.truncated_normal(jax.random.fold_in(key, 102), -6.0, 6.0, grid_shape, jnp.float32)
    return (base_queries, base_keys)


def draw_queries(key, part):
    return query_key_pair(key)[0].astype(jnp.bfloat16)


def draw_keys(key, part):
    return query_key_pair(key)[1].astype(jnp.bfloat16)


def draw_fold_cols(key, part):
    columns = jnp.arange(NLON, dtype=jnp.int32)
    block_index = columns // TW
    within = columns % TW
    segment = block_index * 3 + (within >= 4).astype(jnp.int32) + (within >= TW - 4).astype(jnp.int32)
    offset_start = jnp.where(within < 4, 0, jnp.where(within < TW - 4, 4, TW - 4))
    block_count = NLON // TW
    target_block = (block_index + block_count // 2) % block_count
    same_segment = segment[:, None] == segment[None, :]
    result_rows = []
    for pole_side in range(2):
        ranking = jax.random.randint(jax.random.fold_in(key, 201 + pole_side), (NLON,), 0, 1 << 16) * NLON + columns
        position = jnp.sum(same_segment & (ranking[None, :] < ranking[:, None]), axis=1).astype(jnp.int32)
        result_rows.append(target_block * TW + offset_start + position)
    return jnp.stack(result_rows).astype(jnp.int32)


def level_of(rng, shape, cuts, least, top_value):
    def one(axis_at, blocks):
        draws = jax.random.uniform(jax.random.fold_in(jax.random.fold_in(rng, 6), axis_at), (blocks,), jnp.float32, least / len(cuts), top_value / len(cuts))
        return jnp.repeat(jnp.exp(draws), shape[axis_at] // blocks).reshape((-1,) + (1,) * (len(shape) - axis_at - 1))

    factor_of = one(*cuts[0])
    for cut in cuts[1:]:
        factor_of = factor_of * one(*cut)
    return factor_of


def centred(key, dims, scale, most, cuts=(), kind=jnp.bfloat16):
    values = scale * jax.random.normal(key, dims, jnp.float32)
    if cuts:
        values = values * level_of(key, dims, cuts, -0.22, 0.18)
    return jnp.clip(values, -most, most).astype(kind)


def setup_inputs(seed: int = 0) -> dict:
    arg_keys = jax.random.split(jax.random.key(seed), 6)
    return {
        "queries": draw_queries(jax.random.fold_in(arg_keys[5], 71), 0),
        "keys": draw_keys(jax.random.fold_in(arg_keys[5], 71), 0),
        "values": centred(arg_keys[2], (NLAT, NLON, WIDTH), 1.0, 6.0, ((0, 8), (1, 4))),
        "grad_out": centred(arg_keys[3], (NLAT, NLON, WIDTH), 1.0, 6.0, ((0, 8), (1, 4))),
        "fold_cols": draw_fold_cols(jax.random.fold_in(arg_keys[5], 71), 0),
    }


band_rows = 8

def pad_grid(source, fold_cols):
    lat_rows = source.shape[0]
    lon_cols = source.shape[1]
    columns = ((jnp.arange(lon_cols + 2 * RADIUS) - RADIUS) % lon_cols).astype(jnp.int32)
    middle = jnp.take(source, columns, axis=1)
    north_cols = jnp.take(fold_cols[0], columns).astype(jnp.int32)
    south_cols = jnp.take(fold_cols[1], columns).astype(jnp.int32)
    north_rows = jnp.take(source[:RADIUS][::-1], north_cols, axis=1)
    south_rows = jnp.take(source[lat_rows - RADIUS:][::-1], south_cols, axis=1)
    return jnp.concatenate([north_rows, middle, south_rows], axis=0)

def reference(queries, keys, values, grad_out, fold_cols):
    score_scale = HEAD_DIM ** (-0.5)
    lat_rows, lon_cols, features = queries.shape
    key_pad = pad_grid(keys, fold_cols)
    value_pad = pad_grid(values, fold_cols)
    span = 2 * RADIUS + 1
    offsets = [(shift_row, shift_col) for shift_row in range(span) for shift_col in range(span)]
    halo_rows = band_rows + 2 * RADIUS

    def split_heads(array_block):
        return array_block.astype(jnp.float32).reshape(array_block.shape[0], array_block.shape[1], HEADS, HEAD_DIM)

    def nearby(array_block, shift_row, shift_col):
        return array_block[shift_row:shift_row + band_rows, shift_col:shift_col + lon_cols]

    def band_step(running, band_index):
        key_grad, value_grad = running
        first_row = (band_index * band_rows).astype(jnp.int32)
        query_band = split_heads(lax.dynamic_slice_in_dim(queries, first_row, band_rows, 0))
        grad_band = split_heads(lax.dynamic_slice_in_dim(grad_out, first_row, band_rows, 0))
        key_band = split_heads(lax.dynamic_slice_in_dim(key_pad, first_row, halo_rows, 0))
        value_band = split_heads(lax.dynamic_slice_in_dim(value_pad, first_row, halo_rows, 0))
        scores = jnp.stack([lax.optimization_barrier(jnp.sum(query_band * nearby(key_band, shift_row, shift_col), axis=-1)) for shift_row, shift_col in offsets]) * score_scale
        row_max = lax.optimization_barrier(jnp.max(scores, axis=0))
        log_total = row_max + jnp.log(lax.optimization_barrier(jnp.sum(jnp.exp(scores - row_max), axis=0)))
        weights = jnp.exp(scores - log_total)
        dweights = jnp.stack([lax.optimization_barrier(jnp.sum(grad_band * nearby(value_band, shift_row, shift_col), axis=-1)) for shift_row, shift_col in offsets])
        correction = lax.optimization_barrier(jnp.sum(weights * dweights, axis=0))
        dscores = lax.optimization_barrier((weights * (dweights - correction)).astype(jnp.bfloat16)).astype(jnp.float32)
        weights_low = lax.optimization_barrier(weights.astype(jnp.bfloat16)).astype(jnp.float32)
        query_grad = jnp.zeros((band_rows, lon_cols, HEADS, HEAD_DIM), jnp.float32)
        key_part = jnp.zeros((halo_rows, lon_cols + 2 * RADIUS, HEADS, HEAD_DIM), jnp.float32)
        value_part = jnp.zeros((halo_rows, lon_cols + 2 * RADIUS, HEADS, HEAD_DIM), jnp.float32)
        for position, (shift_row, shift_col) in enumerate(offsets):
            query_grad = query_grad + dscores[position][..., None] * nearby(key_band, shift_row, shift_col)
            key_part = key_part.at[shift_row:shift_row + band_rows, shift_col:shift_col + lon_cols].add(dscores[position][..., None] * query_band)
            value_part = value_part.at[shift_row:shift_row + band_rows, shift_col:shift_col + lon_cols].add(weights_low[position][..., None] * grad_band)
        key_slab = lax.dynamic_slice_in_dim(key_grad, first_row, halo_rows, 0) + score_scale * key_part.reshape(halo_rows, lon_cols + 2 * RADIUS, features)
        value_slab = lax.dynamic_slice_in_dim(value_grad, first_row, halo_rows, 0) + value_part.reshape(halo_rows, lon_cols + 2 * RADIUS, features)
        key_grad = lax.dynamic_update_slice_in_dim(key_grad, key_slab, first_row, 0)
        value_grad = lax.dynamic_update_slice_in_dim(value_grad, value_slab, first_row, 0)
        return ((key_grad, value_grad), (score_scale * query_grad).reshape(band_rows, lon_cols, features))
    pad_shape = (lat_rows + 2 * RADIUS, lon_cols + 2 * RADIUS, features)
    start_grads = (jnp.zeros(pad_shape, jnp.float32), jnp.zeros(pad_shape, jnp.float32))
    (key_grad, value_grad), query_grads = lax.scan(band_step, start_grads, jnp.arange(lat_rows // band_rows))
    _, pull_back = jax.vjp(lambda source: pad_grid(source, fold_cols), jnp.zeros((lat_rows, lon_cols, features), jnp.float32))
    grad_keys = pull_back(key_grad)[0]
    grad_values = pull_back(value_grad)[0]
    grad_queries = query_grads.reshape(lat_rows, lon_cols, features)
    return (grad_queries.astype(jnp.bfloat16), grad_keys.astype(jnp.bfloat16), grad_values.astype(jnp.bfloat16))
```

```python
import functools
import math

import jax
import jax.numpy as jnp
from jax import lax
from jax.experimental import pallas as pl
from jax.experimental.pallas import tpu as pltpu
from jax.sharding import PartitionSpec as P

HEAD_DIM = 64
RADIUS = 4
TILE = 16
LANES = 2 * HEAD_DIM
PER_CHUNK = 2

GROUP = 96
CENTER, WEST, EAST = (0, 64), (64, 16), (80, 16)
SLOT = {0: CENTER, -1: WEST, 1: EAST}
BF16 = jnp.bfloat16
F32 = jnp.float32
MESH = pl.DeviceIdType.MESH


def iota(shape, dim):
    return lax.broadcasted_iota(jnp.int32, shape, dim)


def cell_row(cell):
    return jnp.where(cell < 64, cell // 16, (cell - 64) % 16 // 4)


def cell_col(cell):
    side = jnp.where(cell < 80, (cell - 64) % 4, 20 + (cell - 80) % 4)
    return jnp.where(cell < 64, 4 + cell % 16, side)


def dot(a, b, dims):
    return lax.dot_general(a, b, (dims, ((), ())), preferred_element_type=F32)


def kernel(
    lat_count, lon_count, pairs,
    fold, queries, keys, values, grad_out,
    grad_queries, grad_keys, grad_values,
    ext, edge, back, landed, query, gout, total, bias, select, place, turn,
    load_sem, send_sem, recv_sem, back_send_sem, back_recv_sem,
):
    lat = lax.axis_index("lat")
    lon = lax.axis_index("lon")
    half = lon_count // 2
    chunks = pairs // PER_CHUNK
    at_north = lat == 0
    at_south = lat == lat_count - 1

    def loads(pair, which):
        lanes = pl.ds(pl.multiple_of(pair * LANES, LANES), LANES)
        ends = (
            (keys, ext.at[pair, 0, 1:5, 0:64, :]),
            (values, ext.at[pair, 1, 1:5, 0:64, :]),
            (queries, query.at[pair]),
            (grad_out, gout.at[pair]),
        )
        return [
            pltpu.make_async_copy(source.at[:, :, lanes], target, load_sem.at[pair, n])
            for n, (source, target) in enumerate(ends)
            if n // 2 == which
        ]

    for pair in range(pairs):
        for copy in loads(pair, 0):
            copy.start()
    for pair in range(pairs):
        for copy in loads(pair, 1):
            copy.start()

    north = (1, jnp.where(at_north, 0, lat - 1), jnp.where(at_north, half, 0), jnp.where(at_north, 0, 5))
    south = (4, jnp.where(at_south, lat, lat + 1), jnp.where(at_south, half, 0), jnp.where(at_south, 5, 0))
    vertical = []
    for taken, row, shift, lands in (north, south):
        for step in (0, -1, 1):
            device = (row, lax.rem(lon + step + shift + lon_count, lon_count))
            vertical.append((taken, step, device, lands))
    sideways = [(step, (lat, lax.rem(lon + step + lon_count, lon_count))) for step in (-1, 1)]

    barrier = pltpu.get_barrier_semaphore()
    for _, _, device, _ in vertical:
        pl.semaphore_signal(barrier, inc=1, device_id=device, device_id_type=MESH)
    for _, device in sideways:
        pl.semaphore_signal(barrier, inc=1, device_id=device, device_id_type=MESH)

    def span(chunk):
        return pl.ds(chunk * PER_CHUNK, PER_CHUNK)

    def part(buffer, chunk, group, step):
        start, size = SLOT[step]
        return buffer.at[span(chunk), :, group, pl.ds(start, size), :]

    def side(buffer, chunk, step):
        start, size = SLOT[step]
        return buffer.at[span(chunk), :, 1:5, pl.ds(start, size), :]

    def slot_index(group_is_south, step):
        return 3 * group_is_south + {0: 0, -1: 1, 1: 2}[step]

    def sends(chunk, outgoing, incoming, send, recv, first):
        copies = []
        for n, (step, device) in enumerate(sideways):
            source = edge.at[span(chunk), :, n] if first else side(outgoing, chunk, step)
            copies.append(pltpu.make_async_remote_copy(
                src_ref=source, dst_ref=side(incoming, chunk, -step),
                send_sem=send.at[chunk, 6 + n], recv_sem=recv.at[chunk, 7 - n],
                device_id=device, device_id_type=MESH,
            ))
        for n, (taken, step, device, lands) in enumerate(vertical):
            if not first:
                source = part(outgoing, chunk, 0 if taken == 1 else 5, step)
            elif step == 0:
                source = part(outgoing, chunk, taken, 0)
            else:
                source = edge.at[span(chunk), :, 0 if step < 0 else 1, taken - 1]
            copies.append(pltpu.make_async_remote_copy(
                src_ref=source, dst_ref=part(incoming, chunk, lands, -step),
                send_sem=send.at[chunk, n],
                recv_sem=recv.at[chunk, slot_index(lands // 5, -step)],
                device_id=device, device_id_type=MESH,
            ))
        return copies

    def arrivals(chunk, incoming, send, recv):
        copies = []
        for n, (step, device) in enumerate(sideways):
            ref = side(incoming, chunk, step)
            copies.append(pltpu.make_async_remote_copy(
                src_ref=ref, dst_ref=ref, send_sem=send.at[chunk, 6 + n],
                recv_sem=recv.at[chunk, 6 + n], device_id=device, device_id_type=MESH,
            ))
        for group in (0, 5):
            for step in (0, -1, 1):
                ref = part(incoming, chunk, group, step)
                n = slot_index(group // 5, step)
                copies.append(pltpu.make_async_remote_copy(
                    src_ref=ref, dst_ref=ref, send_sem=send.at[chunk, n],
                    recv_sem=recv.at[chunk, n],
                    device_id=sideways[0][1], device_id_type=MESH,
                ))
        return copies

    row = iota((128, 256), 0)
    col = iota((128, 256), 1)
    wanted = (row % 64 // 4) * 16 + row % 4 + jnp.where(row < 64, 0, 12)
    select[...] = (col == wanted).astype(F32).astype(BF16)

    pl.semaphore_wait(barrier, 8)

    def pack(chunk, carry):
        for inner in range(PER_CHUNK):
            pair = chunk * PER_CHUNK + inner
            for copy in loads(pair, 0):
                copy.wait()
            for kind in range(2):
                cells = ext[pair, kind, 1:5, 0:64, :].reshape(256, LANES)
                packed = dot(select[...], cells, ((1,), (0,))).astype(BF16)
                edge[pair, kind] = packed.reshape(2, 4, 16, LANES)
        for copy in sends(chunk, ext, ext, send_sem, recv_sem, True):
            copy.start()
        return carry

    lax.fori_loop(0, chunks, pack, 0)

    key = iota((4 * GROUP, 128), 0)
    asker = iota((4 * GROUP, 128), 1)
    row_gap = key // GROUP * 4 + cell_row(key % GROUP) - RADIUS - asker // 16
    col_gap = cell_col(key % GROUP) - RADIUS - asker % 16
    seen = (jnp.abs(row_gap) <= RADIUS) & (jnp.abs(col_gap) <= RADIUS)
    bias[...] = jnp.where(seen, 0.0, -1e30)

    row = iota((256, 192), 0)
    col = iota((256, 192), 1)
    target = jnp.clip(col // 32 - 1, 0, 3) * 64 + (col % 16 // 4) * 16 + col % 4
    target = target + jnp.where(col % 32 < 16, 0, 12)
    place[...] = (row == target).astype(F32).astype(BF16)

    @pl.when(at_north | at_south)
    def _():
        row = iota((GROUP, GROUP), 0)
        col = iota((GROUP, GROUP), 1)
        padded_col = cell_col(row)
        source_col = jnp.zeros((GROUP, GROUP), jnp.int32)
        pole = jnp.where(at_north, 0, 1)
        for place_col in range(TILE + 2 * RADIUS):
            grid_col = lax.rem(
                lon * TILE + (place_col - RADIUS) + lon_count * TILE, lon_count * TILE
            )
            within = fold[pole, grid_col] % TILE
            within = within + (-8 if place_col < 4 else 4 if place_col < 20 else 20) - (
                4 if place_col < 4 else 0
            )
            source_col = jnp.where(padded_col == place_col, within, source_col)
        hit = (cell_col(col) == source_col) & (cell_row(col) == 3 - cell_row(row))
        turn[...] = hit.astype(F32).astype(BF16)

    pole_group = jnp.where(at_north, 0, 5)
    low = iota((128, LANES), 1) < HEAD_DIM
    rate = HEAD_DIM ** -0.5
    exponent = rate * math.log2(math.e)

    def by_head(cells):
        zero = jnp.zeros_like(cells)
        return jnp.concatenate([jnp.where(low, cells, zero), jnp.where(low, zero, cells)], axis=0)

    def attend(pair, tile):
        seen_keys = ext[pair, 0, 2 * tile : 2 * tile + 4].reshape(4 * GROUP, LANES)
        seen_values = ext[pair, 1, 2 * tile : 2 * tile + 4].reshape(4 * GROUP, LANES)
        asking = by_head(query[pair, 2 * tile : 2 * tile + 2].reshape(128, LANES))
        grads = by_head(gout[pair, 2 * tile : 2 * tile + 2].reshape(128, LANES))
        outside = jnp.concatenate([bias[...], bias[...]], axis=1)
        scores = dot(seen_keys, asking, ((1,), (1,))) + outside
        top = jnp.max(scores, axis=0, keepdims=True)
        raised = jnp.exp2((scores - top) * exponent)
        weights = raised * (1.0 / jnp.sum(raised, axis=0, keepdims=True))
        dweights = dot(seen_values, grads, ((1,), (1,)))
        correction = jnp.sum(weights * dweights, axis=0, keepdims=True)
        dscores = (weights * (dweights - correction)).astype(BF16)
        dkey = dot(dscores, asking, ((1,), (0,))) * rate
        dvalue = dot(weights.astype(BF16), grads, ((1,), (0,)))
        dquery = dot(dscores, seen_keys, ((0,), (0,)))
        dquery = jnp.where(low, dquery[:128], dquery[128:]) * rate
        lanes = pl.ds(pl.multiple_of(pair * LANES, LANES), LANES)
        grad_queries[128 * tile : 128 * tile + 128, lanes] = dquery.astype(BF16)
        return dkey, dvalue

    def turn_pole(buffer, chunk, dims):
        @pl.when(at_north | at_south)
        def _():
            for inner in range(PER_CHUNK):
                pair = chunk * PER_CHUNK + inner
                both = jnp.concatenate(
                    [buffer[pair, 0, pole_group], buffer[pair, 1, pole_group]], axis=1
                )
                turned = dot(turn[...], both, dims).astype(BF16)
                buffer[pair, 0, pole_group] = turned[:, :LANES]
                buffer[pair, 1, pole_group] = turned[:, LANES:]

    def work(chunk, carry):
        for inner in range(PER_CHUNK):
            for copy in loads(chunk * PER_CHUNK + inner, 1):
                copy.wait()
        for copy in arrivals(chunk, ext, send_sem, recv_sem):
            copy.wait_recv()
        turn_pole(ext, chunk, ((1,), (0,)))
        for inner in range(PER_CHUNK):
            pair = chunk * PER_CHUNK + inner
            upper = attend(pair, 0)
            lower = attend(pair, 1)
            for kind in range(2):
                whole = jnp.concatenate(
                    [
                        upper[kind][: 2 * GROUP],
                        upper[kind][2 * GROUP :] + lower[kind][: 2 * GROUP],
                        lower[kind][2 * GROUP :],
                    ],
                    axis=0,
                ).reshape(6, GROUP, LANES)
                back[pair, kind] = whole.astype(BF16)
                total[pair, kind] = whole[1:5, 0:64].reshape(256, LANES)
        turn_pole(back, chunk, ((0,), (0,)))
        for copy in sends(chunk, back, landed, back_send_sem, back_recv_sem, False):
            copy.start()
        return carry

    lax.fori_loop(0, chunks, work, 0)

    def finish(chunk, carry):
        for copy in arrivals(chunk, landed, back_send_sem, back_recv_sem):
            copy.wait_recv()
        for inner in range(PER_CHUNK):
            pair = chunk * PER_CHUNK + inner
            lanes = pl.ds(pl.multiple_of(pair * LANES, LANES), LANES)
            for kind, out in ((0, grad_keys), (1, grad_values)):
                sides = landed[pair, kind, :, 64:96, :].reshape(192, LANES)
                whole = total[pair, kind] + dot(place[...], sides, ((1,), (0,)))
                first = whole[:64] + landed[pair, kind, 0, 0:64, :].astype(F32)
                last = whole[192:] + landed[pair, kind, 5, 0:64, :].astype(F32)
                out[0:64, lanes] = first.astype(BF16)
                out[64:192, lanes] = whole[64:192].astype(BF16)
                out[192:256, lanes] = last.astype(BF16)
        return carry

    lax.fori_loop(0, chunks, finish, 0)

    def drain(chunk, carry):
        for copy in sends(chunk, ext, ext, send_sem, recv_sem, True):
            copy.wait_send()
        for copy in sends(chunk, back, landed, back_send_sem, back_recv_sem, False):
            copy.wait_send()
        return carry

    lax.fori_loop(0, chunks, drain, 0)


def on_device(lat_count, lon_count, queries, keys, values, grad_out, fold_cols):
    height, breadth, features = queries.shape
    pairs = features // LANES
    chunks = pairs // PER_CHUNK
    cells = height * breadth
    inputs = [a.reshape(4, 64, features) for a in (queries, keys, values, grad_out)]
    window = (pairs, 2, 6, GROUP, LANES)
    out = jax.ShapeDtypeStruct((cells, features), BF16)
    results = pl.pallas_call(
        functools.partial(kernel, lat_count, lon_count, pairs),
        out_shape=(out, out, out),
        in_specs=[pl.BlockSpec(memory_space=pltpu.SMEM)]
        + [pl.BlockSpec(memory_space=pl.ANY)] * 4,
        out_specs=[pl.BlockSpec(memory_space=pltpu.VMEM)] * 3,
        scratch_shapes=[
            pltpu.VMEM(window, BF16),
            pltpu.VMEM((pairs, 2, 2, 4, 16, LANES), BF16),
            pltpu.VMEM(window, BF16),
            pltpu.VMEM(window, BF16),
            pltpu.VMEM((pairs, 4, 64, LANES), BF16),
            pltpu.VMEM((pairs, 4, 64, LANES), BF16),
            pltpu.VMEM((pairs, 2, cells, LANES), F32),
            pltpu.VMEM((4 * GROUP, 128), F32),
            pltpu.VMEM((128, 256), BF16),
            pltpu.VMEM((256, 192), BF16),
            pltpu.VMEM((GROUP, GROUP), BF16),
            pltpu.SemaphoreType.DMA((pairs, 4)),
        ]
        + [pltpu.SemaphoreType.DMA((chunks, 8))] * 4,
        compiler_params=pltpu.CompilerParams(
            collective_id=0, has_side_effects=True, vmem_limit_bytes=44 << 20
        ),
        cost_estimate=pl.CostEstimate(
            flops=2_000_000_000, bytes_accessed=4_000_000, transcendentals=1_600_000
        ),
    )(fold_cols, *inputs)
    return tuple(r.reshape(height, breadth, features) for r in results)


def solution(mesh):
    block = P("lat", "lon", None)
    return jax.shard_map(
        functools.partial(on_device, mesh.shape["lat"], mesh.shape["lon"]),
        mesh=mesh,
        in_specs=(block, block, block, block, P()),
        out_specs=(block, block, block),
        check_vma=False,
    )
```

```python
import functools
import math

import jax
import jax.numpy as jnp
from jax import lax
from jax.experimental import pallas as pl
from jax.experimental.pallas import tpu as pltpu
from jax.sharding import PartitionSpec as P

HEAD_DIM = 64
RADIUS = 4
TILE = 16
LANES = 2 * HEAD_DIM
PER_CHUNK = 2

GROUP = 96
CENTER, WEST, EAST = (0, 64), (64, 16), (80, 16)
SLOT = {0: CENTER, -1: WEST, 1: EAST}
BF16 = jnp.bfloat16
F32 = jnp.float32
MESH = pl.DeviceIdType.MESH


def iota(shape, dim):
    return lax.broadcasted_iota(jnp.int32, shape, dim)


def cell_row(cell):
    return jnp.where(cell < 64, cell // 16, (cell - 64) % 16 // 4)


def cell_col(cell):
    side = jnp.where(cell < 80, (cell - 64) % 4, 20 + (cell - 80) % 4)
    return jnp.where(cell < 64, 4 + cell % 16, side)


def dot(a, b, dims):
    return lax.dot_general(a, b, (dims, ((), ())), preferred_element_type=F32)


def kernel(
    lat_count, lon_count, pairs,
    fold, queries, keys, values, grad_out,
    grad_queries, grad_keys, grad_values,
    ext, edge, back, landed, query, gout, total, bias, select, place, turn,
    load_sem, send_sem, recv_sem, back_send_sem, back_recv_sem,
):
    lat = lax.axis_index("lat")
    lon = lax.axis_index("lon")
    half = lon_count // 2
    chunks = pairs // PER_CHUNK
    at_north = lat == 0
    at_south = lat == lat_count - 1

    def loads(pair, which):
        lanes = pl.ds(pl.multiple_of(pair * LANES, LANES), LANES)
        ends = (
            (keys, ext.at[pair, 0, 1:5, 0:64, :]),
            (values, ext.at[pair, 1, 1:5, 0:64, :]),
            (queries, query.at[pair]),
            (grad_out, gout.at[pair]),
        )
        return [
            pltpu.make_async_copy(source.at[:, :, lanes], target, load_sem.at[pair, n])
            for n, (source, target) in enumerate(ends)
            if n // 2 == which
        ]

    for pair in range(pairs):
        for copy in loads(pair, 0):
            copy.start()
    for pair in range(pairs):
        for copy in loads(pair, 1):
            copy.start()

    directions = (
        (1, 0, 0, at_north, 5, jnp.where(at_north, 0, lat - 1)),
        (4, 5, 5, at_south, 0, jnp.where(at_south, lat, lat + 1)),
    )

    def around(step):
        return lax.rem(lon + step + lon_count, lon_count)

    sideways = [(step, (lat, around(step))) for step in (-1, 1)]

    barrier = pltpu.get_barrier_semaphore()
    for _, _, _, polar, _, row in directions:
        pl.semaphore_signal(
            barrier, inc=1, device_id=(row, jnp.where(polar, around(half), lon)),
            device_id_type=MESH,
        )
    for _, device in sideways:
        pl.semaphore_signal(barrier, inc=1, device_id=device, device_id_type=MESH)

    @pl.when(at_north | at_south)
    def _():
        for step in (-1, 1):
            pl.semaphore_signal(
                barrier, inc=1, device_id=(lat, around(step + half)), device_id_type=MESH
            )

    def span(chunk):
        return pl.ds(chunk * PER_CHUNK, PER_CHUNK)

    def part(buffer, chunk, group, step):
        start, size = SLOT[step]
        return buffer.at[span(chunk), :, group, pl.ds(start, size), :]

    def side(buffer, chunk, step):
        start, size = SLOT[step]
        return buffer.at[span(chunk), :, 1:5, pl.ds(start, size), :]

    def slot_index(group_is_south, step):
        return 3 * group_is_south + {0: 0, -1: 1, 1: 2}[step]

    def remote(source, target, send, recv, device):
        return pltpu.make_async_remote_copy(
            src_ref=source, dst_ref=target, send_sem=send, recv_sem=recv,
            device_id=device, device_id_type=MESH,
        )

    def stage(first):
        if first:
            return ext, ext, send_sem, recv_sem
        return back, landed, back_send_sem, back_recv_sem

    def send_sideways(chunk, first):
        outgoing, incoming, send, recv = stage(first)
        for n, (step, device) in enumerate(sideways):
            source = edge.at[span(chunk), :, n] if first else side(outgoing, chunk, step)
            remote(
                source, side(incoming, chunk, -step),
                send.at[chunk, 6 + n], recv.at[chunk, 7 - n], device,
            ).start()

    def send_rows(chunk, first):
        outgoing, incoming, send, recv = stage(first)
        for n, (taken, halo, across, polar, lands, row) in enumerate(directions):
            group = jnp.where(polar, across, lands)
            remote(
                part(outgoing, chunk, taken if first else halo, 0),
                part(incoming, chunk, group, 0),
                send.at[chunk, 3 * n], recv.at[chunk, slot_index(group // 5, 0)],
                (row, jnp.where(polar, around(half), lon)),
            ).start()

    def send_corners_across(chunk, first):
        outgoing, incoming, send, recv = stage(first)
        for n, (taken, halo, across, polar, lands, row) in enumerate(directions):
            @pl.when(polar)
            def _():
                for step in (-1, 1):
                    if first:
                        source = edge.at[span(chunk), :, 0 if step < 0 else 1, taken - 1]
                    else:
                        source = part(outgoing, chunk, halo, step)
                    remote(
                        source, part(incoming, chunk, across, -step),
                        send.at[chunk, slot_index(n, step)],
                        recv.at[chunk, slot_index(across // 5, -step)],
                        (lat, around(step + half)),
                    ).start()

    def send_corners(chunk, first):
        outgoing, incoming, send, recv = stage(first)
        for n, (taken, halo, across, polar, lands, row) in enumerate(directions):
            @pl.when(jnp.logical_not(polar))
            def _():
                for step in (-1, 1):
                    remote(
                        part(outgoing, chunk, taken if first else halo, step),
                        part(incoming, chunk, lands, step),
                        send.at[chunk, slot_index(n, step)],
                        recv.at[chunk, slot_index(lands // 5, step)],
                        (row, lon),
                    ).start()

    def side_ends(chunk, first):
        outgoing, incoming, send, recv = stage(first)
        copies = []
        for n, (step, device) in enumerate(sideways):
            ref = side(incoming, chunk, step)
            copies.append(remote(ref, ref, send.at[chunk, 6 + n], recv.at[chunk, 6 + n], device))
        return copies

    def part_ends(chunk, first, group, steps):
        outgoing, incoming, send, recv = stage(first)
        copies = []
        for step in steps:
            ref = part(incoming, chunk, group, step)
            n = slot_index(group // 5, step)
            copies.append(
                remote(ref, ref, send.at[chunk, n], recv.at[chunk, n], sideways[0][1])
            )
        return copies

    row = iota((128, 256), 0)
    col = iota((128, 256), 1)
    wanted = (row % 64 // 4) * 16 + row % 4 + jnp.where(row < 64, 0, 12)
    select[...] = (col == wanted).astype(F32).astype(BF16)

    pl.semaphore_wait(barrier, jnp.where(at_north | at_south, 6, 4))

    def pack(chunk, carry):
        for inner in range(PER_CHUNK):
            pair = chunk * PER_CHUNK + inner
            for copy in loads(pair, 0):
                copy.wait()
            for kind in range(2):
                cells = ext[pair, kind, 1:5, 0:64, :].reshape(256, LANES)
                packed = dot(select[...], cells, ((1,), (0,))).astype(BF16)
                edge[pair, kind] = packed.reshape(2, 4, 16, LANES)
        send_sideways(chunk, True)
        send_corners_across(chunk, True)
        send_rows(chunk, True)
        return carry

    lax.fori_loop(0, chunks, pack, 0)

    key = iota((4 * GROUP, 128), 0)
    asker = iota((4 * GROUP, 128), 1)
    row_gap = key // GROUP * 4 + cell_row(key % GROUP) - RADIUS - asker // 16
    col_gap = cell_col(key % GROUP) - RADIUS - asker % 16
    seen = (jnp.abs(row_gap) <= RADIUS) & (jnp.abs(col_gap) <= RADIUS)
    bias[...] = jnp.where(seen, 0.0, -1e30)

    row = iota((256, 192), 0)
    col = iota((256, 192), 1)
    target = jnp.clip(col // 32 - 1, 0, 3) * 64 + (col % 16 // 4) * 16 + col % 4
    target = target + jnp.where(col % 32 < 16, 0, 12)
    direct = ((col >= 32) | at_north) & ((col < 160) | at_south)
    place[...] = ((row == target) & direct).astype(F32).astype(BF16)

    @pl.when(at_north | at_south)
    def _():
        row = iota((GROUP, GROUP), 0)
        col = iota((GROUP, GROUP), 1)
        padded_col = cell_col(row)
        source_col = jnp.zeros((GROUP, GROUP), jnp.int32)
        pole = jnp.where(at_north, 0, 1)
        for place_col in range(TILE + 2 * RADIUS):
            grid_col = lax.rem(
                lon * TILE + (place_col - RADIUS) + lon_count * TILE, lon_count * TILE
            )
            within = fold[pole, grid_col] % TILE
            within = within + (-8 if place_col < 4 else 4 if place_col < 20 else 20) - (
                4 if place_col < 4 else 0
            )
            source_col = jnp.where(padded_col == place_col, within, source_col)
        hit = (cell_col(col) == source_col) & (cell_row(col) == 3 - cell_row(row))
        turn[...] = hit.astype(F32).astype(BF16)

    pole_group = jnp.where(at_north, 0, 5)
    low = iota((128, LANES), 1) < HEAD_DIM
    rate = HEAD_DIM ** -0.5
    exponent = rate * math.log2(math.e)

    def by_head(cells):
        zero = jnp.zeros_like(cells)
        return jnp.concatenate([jnp.where(low, cells, zero), jnp.where(low, zero, cells)], axis=0)

    def attend(pair, tile):
        seen_keys = ext[pair, 0, 2 * tile : 2 * tile + 4].reshape(4 * GROUP, LANES)
        seen_values = ext[pair, 1, 2 * tile : 2 * tile + 4].reshape(4 * GROUP, LANES)
        asking = by_head(query[pair, 2 * tile : 2 * tile + 2].reshape(128, LANES))
        grads = by_head(gout[pair, 2 * tile : 2 * tile + 2].reshape(128, LANES))
        outside = jnp.concatenate([bias[...], bias[...]], axis=1)
        scores = dot(seen_keys, asking, ((1,), (1,))) + outside
        top = jnp.max(scores, axis=0, keepdims=True)
        raised = jnp.exp2((scores - top) * exponent)
        weights = raised * (1.0 / jnp.sum(raised, axis=0, keepdims=True))
        dweights = dot(seen_values, grads, ((1,), (1,)))
        correction = jnp.sum(weights * dweights, axis=0, keepdims=True)
        dscores = (weights * (dweights - correction)).astype(BF16)
        dkey = dot(dscores, asking, ((1,), (0,))) * rate
        dvalue = dot(weights.astype(BF16), grads, ((1,), (0,)))
        dquery = dot(dscores, seen_keys, ((0,), (0,)))
        dquery = jnp.where(low, dquery[:128], dquery[128:]) * rate
        lanes = pl.ds(pl.multiple_of(pair * LANES, LANES), LANES)
        grad_queries[128 * tile : 128 * tile + 128, lanes] = dquery.astype(BF16)
        return dkey, dvalue

    def turn_pole(buffer, chunk, dims):
        @pl.when(at_north | at_south)
        def _():
            for inner in range(PER_CHUNK):
                pair = chunk * PER_CHUNK + inner
                both = jnp.concatenate(
                    [buffer[pair, 0, pole_group], buffer[pair, 1, pole_group]], axis=1
                )
                turned = dot(turn[...], both, dims).astype(BF16)
                buffer[pair, 0, pole_group] = turned[:, :LANES]
                buffer[pair, 1, pole_group] = turned[:, LANES:]

    def pass_on(chunk):
        for copy in side_ends(chunk, True):
            copy.wait_recv()
        send_corners(chunk, True)

    def pass_back(chunk):
        for group, inward, polar in ((0, 1, at_north), (5, 4, at_south)):
            @pl.when(jnp.logical_not(polar))
            def _():
                for copy in part_ends(chunk, False, group, (-1, 1)):
                    copy.wait_recv()
                pairs_here = span(chunk)
                own = back[pairs_here, :, inward, 64:96, :].astype(F32)
                more = landed[pairs_here, :, group, 64:96, :].astype(F32)
                back[pairs_here, :, inward, 64:96, :] = (own + more).astype(BF16)
        send_sideways(chunk, False)

    pass_on(0)

    def work(chunk, carry):
        for inner in range(PER_CHUNK):
            for copy in loads(chunk * PER_CHUNK + inner, 1):
                copy.wait()
        for group in (0, 5):
            for copy in part_ends(chunk, True, group, (0, -1, 1)):
                copy.wait_recv()
        turn_pole(ext, chunk, ((1,), (0,)))
        for inner in range(PER_CHUNK):
            pair = chunk * PER_CHUNK + inner
            upper = attend(pair, 0)
            lower = attend(pair, 1)
            for kind in range(2):
                whole = jnp.concatenate(
                    [
                        upper[kind][: 2 * GROUP],
                        upper[kind][2 * GROUP :] + lower[kind][: 2 * GROUP],
                        lower[kind][2 * GROUP :],
                    ],
                    axis=0,
                ).reshape(6, GROUP, LANES)
                back[pair, kind] = whole.astype(BF16)
                total[pair, kind] = whole[1:5, 0:64].reshape(256, LANES)
            if inner == 0:
                @pl.when(chunk + 1 < chunks)
                def _():
                    pass_on(chunk + 1)

                @pl.when(chunk > 0)
                def _():
                    pass_back(chunk - 1)

        turn_pole(back, chunk, ((0,), (0,)))
        send_corners(chunk, False)
        send_corners_across(chunk, False)
        send_rows(chunk, False)
        return carry

    lax.fori_loop(0, chunks, work, 0)
    pass_back(chunks - 1)

    def finish(chunk, carry):
        for copy in side_ends(chunk, False):
            copy.wait_recv()
        for group, polar in ((0, at_north), (5, at_south)):
            for copy in part_ends(chunk, False, group, (0,)):
                copy.wait_recv()

            @pl.when(polar)
            def _():
                for copy in part_ends(chunk, False, group, (-1, 1)):
                    copy.wait_recv()
        for inner in range(PER_CHUNK):
            pair = chunk * PER_CHUNK + inner
            lanes = pl.ds(pl.multiple_of(pair * LANES, LANES), LANES)
            for kind, out in ((0, grad_keys), (1, grad_values)):
                sides = landed[pair, kind, :, 64:96, :].reshape(192, LANES)
                whole = total[pair, kind] + dot(place[...], sides, ((1,), (0,)))
                first = whole[:64] + landed[pair, kind, 0, 0:64, :].astype(F32)
                last = whole[192:] + landed[pair, kind, 5, 0:64, :].astype(F32)
                out[0:64, lanes] = first.astype(BF16)
                out[64:192, lanes] = whole[64:192].astype(BF16)
                out[192:256, lanes] = last.astype(BF16)
        return carry

    lax.fori_loop(0, chunks, finish, 0)

    def drain(chunk, carry):
        for first in (True, False):
            for copy in side_ends(chunk, first):
                copy.wait_send()
            for group in (0, 5):
                for copy in part_ends(chunk, first, group, (0, -1, 1)):
                    copy.wait_send()
        return carry

    lax.fori_loop(0, chunks, drain, 0)


def on_device(lat_count, lon_count, queries, keys, values, grad_out, fold_cols):
    height, breadth, features = queries.shape
    pairs = features // LANES
    chunks = pairs // PER_CHUNK
    cells = height * breadth
    inputs = [a.reshape(4, 64, features) for a in (queries, keys, values, grad_out)]
    window = (pairs, 2, 6, GROUP, LANES)
    out = jax.ShapeDtypeStruct((cells, features), BF16)
    results = pl.pallas_call(
        functools.partial(kernel, lat_count, lon_count, pairs),
        out_shape=(out, out, out),
        in_specs=[pl.BlockSpec(memory_space=pltpu.SMEM)]
        + [pl.BlockSpec(memory_space=pl.ANY)] * 4,
        out_specs=[pl.BlockSpec(memory_space=pltpu.VMEM)] * 3,
        scratch_shapes=[
            pltpu.VMEM(window, BF16),
            pltpu.VMEM((pairs, 2, 2, 4, 16, LANES), BF16),
            pltpu.VMEM(window, BF16),
            pltpu.VMEM(window, BF16),
            pltpu.VMEM((pairs, 4, 64, LANES), BF16),
            pltpu.VMEM((pairs, 4, 64, LANES), BF16),
            pltpu.VMEM((pairs, 2, cells, LANES), F32),
            pltpu.VMEM((4 * GROUP, 128), F32),
            pltpu.VMEM((128, 256), BF16),
            pltpu.VMEM((256, 192), BF16),
            pltpu.VMEM((GROUP, GROUP), BF16),
            pltpu.SemaphoreType.DMA((pairs, 4)),
        ]
        + [pltpu.SemaphoreType.DMA((chunks, 8))] * 4,
        compiler_params=pltpu.CompilerParams(
            collective_id=0, has_side_effects=True, vmem_limit_bytes=60 << 20
        ),
        cost_estimate=pl.CostEstimate(
            flops=2_000_000_000, bytes_accessed=4_000_000, transcendentals=1_600_000
        ),
    )(fold_cols, *inputs)
    return tuple(r.reshape(height, breadth, features) for r in results)


def solution(mesh):
    block = P("lat", "lon", None)
    return jax.shard_map(
        functools.partial(on_device, mesh.shape["lat"], mesh.shape["lon"]),
        mesh=mesh,
        in_specs=(block, block, block, block, P()),
        out_specs=(block, block, block),
        check_vma=False,
    )
```

```python
import functools
import math

import jax
import jax.numpy as jnp
from jax import lax
from jax.experimental import pallas as pl
from jax.experimental.pallas import tpu as pltpu
from jax.sharding import PartitionSpec as P

HEAD_DIM = 64
RADIUS = 4
TILE = 16
LANES = 2 * HEAD_DIM
PER_CHUNK = 2
FIRST_ALONG = False

GROUP = 96
CENTER, WEST, EAST = (0, 64), (64, 16), (80, 16)
SLOT = {0: CENTER, -1: WEST, 1: EAST}
BF16 = jnp.bfloat16
F32 = jnp.float32
MESH = pl.DeviceIdType.MESH


def iota(shape, dim):
    return lax.broadcasted_iota(jnp.int32, shape, dim)


def cell_row(cell):
    return jnp.where(cell < 64, cell // 16, (cell - 64) % 16 // 4)


def cell_col(cell):
    side = jnp.where(cell < 80, (cell - 64) % 4, 20 + (cell - 80) % 4)
    return jnp.where(cell < 64, 4 + cell % 16, side)


def dot(a, b, dims):
    return lax.dot_general(a, b, (dims, ((), ())), preferred_element_type=F32)


def kernel(
    lat_count, lon_count, pairs,
    fold, queries, keys, values, grad_out,
    grad_queries, grad_keys, grad_values,
    ext, edge, back, landed, query, gout, total, bias, select, place, turn, hop,
    load_sem, send_sem, recv_sem, back_send_sem, back_recv_sem, hop_send_sem, hop_recv_sem,
):
    lat = lax.axis_index("lat")
    lon = lax.axis_index("lon")
    half = lon_count // 2
    chunks = pairs // PER_CHUNK
    at_north = lat == 0
    at_south = lat == lat_count - 1

    def loads(pair, which):
        lanes = pl.ds(pl.multiple_of(pair * LANES, LANES), LANES)
        ends = (
            (keys, ext.at[pair, 0, 1:5, 0:64, :]),
            (values, ext.at[pair, 1, 1:5, 0:64, :]),
            (queries, query.at[pair]),
            (grad_out, gout.at[pair]),
        )
        return [
            pltpu.make_async_copy(source.at[:, :, lanes], target, load_sem.at[pair, n])
            for n, (source, target) in enumerate(ends)
            if n // 2 == which
        ]

    for pair in range(pairs):
        for copy in loads(pair, 0):
            copy.start()
    for pair in range(pairs):
        for copy in loads(pair, 1):
            copy.start()

    directions = (
        (1, 0, 0, at_north, 5, jnp.where(at_north, 0, lat - 1)),
        (4, 5, 5, at_south, 0, jnp.where(at_south, lat, lat + 1)),
    )

    def around(step):
        return lax.rem(lon + step + lon_count, lon_count)

    relays = lat == 2
    relays = relays | (lat == lat_count - 3)
    at_pole = at_north | at_south
    relay_row = jnp.where(at_north, 2, lat_count - 3)
    pole_row = jnp.where(lat == 2, 0, lat_count - 1)
    to_relay = half if FIRST_ALONG else 0
    from_relay = 0 if FIRST_ALONG else half

    sideways = [(step, (lat, around(step))) for step in (-1, 1)]

    barrier = pltpu.get_barrier_semaphore()
    for _, _, _, polar, _, row in directions:
        pl.semaphore_signal(
            barrier, inc=1, device_id=(row, jnp.where(polar, around(half), lon)),
            device_id_type=MESH,
        )
    for _, device in sideways:
        pl.semaphore_signal(barrier, inc=1, device_id=device, device_id_type=MESH)

    @pl.when(at_north | at_south)
    def _():
        for step in (-1, 1):
            pl.semaphore_signal(
                barrier, inc=1, device_id=(lat, around(step + half)), device_id_type=MESH
            )
        for step in (0, half):
            pl.semaphore_signal(
                barrier, inc=1, device_id=(relay_row, around(step)), device_id_type=MESH
            )

    @pl.when(relays)
    def _():
        for step in (0, half):
            pl.semaphore_signal(
                barrier, inc=1, device_id=(pole_row, around(step)), device_id_type=MESH
            )

    def span(chunk):
        return pl.ds(chunk * PER_CHUNK, PER_CHUNK)

    def part(buffer, chunk, group, step):
        start, size = SLOT[step]
        return buffer.at[span(chunk), :, group, pl.ds(start, size), :]

    def side(buffer, chunk, step):
        start, size = SLOT[step]
        return buffer.at[span(chunk), :, 1:5, pl.ds(start, size), :]

    def slot_index(group_is_south, step):
        return 3 * group_is_south + {0: 0, -1: 1, 1: 2}[step]

    def remote(source, target, send, recv, device):
        return pltpu.make_async_remote_copy(
            src_ref=source, dst_ref=target, send_sem=send, recv_sem=recv,
            device_id=device, device_id_type=MESH,
        )

    def stage(first):
        if first:
            return ext, ext, send_sem, recv_sem
        return back, landed, back_send_sem, back_recv_sem

    def send_sideways(chunk, first):
        outgoing, incoming, send, recv = stage(first)
        for n, (step, device) in enumerate(sideways):
            source = edge.at[span(chunk), :, n] if first else side(outgoing, chunk, step)
            remote(
                source, side(incoming, chunk, -step),
                send.at[chunk, 6 + n], recv.at[chunk, 7 - n], device,
            ).start()

    def send_rows(chunk, first):
        outgoing, incoming, send, recv = stage(first)
        for n, (taken, halo, across, polar, lands, row) in enumerate(directions):
            group = taken if first else halo

            @pl.when(jnp.logical_not(polar))
            def _():
                remote(
                    part(outgoing, chunk, group, 0), part(incoming, chunk, lands, 0),
                    send.at[chunk, 3 * n], recv.at[chunk, slot_index(lands // 5, 0)], (row, lon),
                ).start()

            @pl.when(polar)
            def _():
                if first:
                    remote(
                        rows_of(outgoing, chunk, 1, group), hop.at[span(chunk)],
                        send.at[chunk, 8], hop_recv_sem.at[chunk],
                        (relay_row, around(to_relay)),
                    ).start()
                else:
                    remote(
                        rows_of(outgoing, chunk, 1, group), rows_of(incoming, chunk, 1, across),
                        send.at[chunk, 8], recv.at[chunk, 8], (row, around(half)),
                    ).start()
                remote(
                    rows_of(outgoing, chunk, 0, group), rows_of(incoming, chunk, 0, across),
                    send.at[chunk, 3 * n], recv.at[chunk, 3 * n], (row, around(half)),
                ).start()

    def rows_of(buffer, chunk, kind, group):
        return buffer.at[span(chunk), kind, group, pl.ds(0, 64), :]

    def relay(chunk):
        @pl.when(relays)
        def _():
            here = hop.at[span(chunk)]
            copy = remote(
                here, rows_of(ext, chunk, 1, jnp.where(lat == 2, 0, 5)),
                hop_send_sem.at[chunk], recv_sem.at[chunk, 8], (pole_row, around(from_relay)),
            )
            remote(
                here, here, hop_send_sem.at[chunk], hop_recv_sem.at[chunk], (pole_row, lon)
            ).wait_recv()
            copy.start()

    def row_ends(chunk, first, wait):
        outgoing, incoming, send, recv = stage(first)
        for n, (taken, halo, across, polar, lands, row) in enumerate(directions):
            @pl.when(jnp.logical_not(polar))
            def _():
                wait(part_ends(chunk, first, across, (0,))[0])

            @pl.when(polar)
            def _():
                for kind, at in ((0, 3 * n), (1, 8)):
                    ref = rows_of(incoming, chunk, kind, across)
                    wait(remote(
                        ref, ref, send.at[chunk, at], recv.at[chunk, at], sideways[0][1]
                    ))

    def send_corners_across(chunk, first):
        outgoing, incoming, send, recv = stage(first)
        for n, (taken, halo, across, polar, lands, row) in enumerate(directions):
            @pl.when(polar)
            def _():
                for step in (-1, 1):
                    if first:
                        source = edge.at[span(chunk), :, 0 if step < 0 else 1, taken - 1]
                    else:
                        source = part(outgoing, chunk, halo, step)
                    remote(
                        source, part(incoming, chunk, across, -step),
                        send.at[chunk, slot_index(n, step)],
                        recv.at[chunk, slot_index(across // 5, -step)],
                        (lat, around(step + half)),
                    ).start()

    def send_corners(chunk, first):
        outgoing, incoming, send, recv = stage(first)
        for n, (taken, halo, across, polar, lands, row) in enumerate(directions):
            @pl.when(jnp.logical_not(polar))
            def _():
                for step in (-1, 1):
                    remote(
                        part(outgoing, chunk, taken if first else halo, step),
                        part(incoming, chunk, lands, step),
                        send.at[chunk, slot_index(n, step)],
                        recv.at[chunk, slot_index(lands // 5, step)],
                        (row, lon),
                    ).start()

    def side_ends(chunk, first):
        outgoing, incoming, send, recv = stage(first)
        copies = []
        for n, (step, device) in enumerate(sideways):
            ref = side(incoming, chunk, step)
            copies.append(remote(ref, ref, send.at[chunk, 6 + n], recv.at[chunk, 6 + n], device))
        return copies

    def part_ends(chunk, first, group, steps):
        outgoing, incoming, send, recv = stage(first)
        copies = []
        for step in steps:
            ref = part(incoming, chunk, group, step)
            n = slot_index(group // 5, step)
            copies.append(
                remote(ref, ref, send.at[chunk, n], recv.at[chunk, n], sideways[0][1])
            )
        return copies

    row = iota((128, 256), 0)
    col = iota((128, 256), 1)
    wanted = (row % 64 // 4) * 16 + row % 4 + jnp.where(row < 64, 0, 12)
    select[...] = (col == wanted).astype(F32).astype(BF16)

    pl.semaphore_wait(barrier, jnp.where(at_pole, 8, jnp.where(relays, 6, 4)))

    def pack(chunk, carry):
        for inner in range(PER_CHUNK):
            pair = chunk * PER_CHUNK + inner
            for copy in loads(pair, 0):
                copy.wait()
            for kind in range(2):
                cells = ext[pair, kind, 1:5, 0:64, :].reshape(256, LANES)
                packed = dot(select[...], cells, ((1,), (0,))).astype(BF16)
                edge[pair, kind] = packed.reshape(2, 4, 16, LANES)
        send_sideways(chunk, True)
        send_rows(chunk, True)
        send_corners_across(chunk, True)
        return carry

    lax.fori_loop(0, chunks, pack, 0)

    key = iota((4 * GROUP, 128), 0)
    asker = iota((4 * GROUP, 128), 1)
    row_gap = key // GROUP * 4 + cell_row(key % GROUP) - RADIUS - asker // 16
    col_gap = cell_col(key % GROUP) - RADIUS - asker % 16
    seen = (jnp.abs(row_gap) <= RADIUS) & (jnp.abs(col_gap) <= RADIUS)
    bias[...] = jnp.where(seen, 0.0, -1e30)

    row = iota((256, 192), 0)
    col = iota((256, 192), 1)
    target = jnp.clip(col // 32 - 1, 0, 3) * 64 + (col % 16 // 4) * 16 + col % 4
    target = target + jnp.where(col % 32 < 16, 0, 12)
    direct = ((col >= 32) | at_north) & ((col < 160) | at_south)
    place[...] = ((row == target) & direct).astype(F32).astype(BF16)

    @pl.when(at_north | at_south)
    def _():
        row = iota((GROUP, GROUP), 0)
        col = iota((GROUP, GROUP), 1)
        padded_col = cell_col(row)
        source_col = jnp.zeros((GROUP, GROUP), jnp.int32)
        pole = jnp.where(at_north, 0, 1)
        for place_col in range(TILE + 2 * RADIUS):
            grid_col = lax.rem(
                lon * TILE + (place_col - RADIUS) + lon_count * TILE, lon_count * TILE
            )
            within = fold[pole, grid_col] % TILE
            within = within + (-8 if place_col < 4 else 4 if place_col < 20 else 20) - (
                4 if place_col < 4 else 0
            )
            source_col = jnp.where(padded_col == place_col, within, source_col)
        hit = (cell_col(col) == source_col) & (cell_row(col) == 3 - cell_row(row))
        turn[...] = hit.astype(F32).astype(BF16)

    pole_group = jnp.where(at_north, 0, 5)
    low = iota((128, LANES), 1) < HEAD_DIM
    rate = HEAD_DIM ** -0.5
    exponent = rate * math.log2(math.e)

    def by_head(cells):
        zero = jnp.zeros_like(cells)
        return jnp.concatenate([jnp.where(low, cells, zero), jnp.where(low, zero, cells)], axis=0)

    def attend(pair, tile):
        seen_keys = ext[pair, 0, 2 * tile : 2 * tile + 4].reshape(4 * GROUP, LANES)
        seen_values = ext[pair, 1, 2 * tile : 2 * tile + 4].reshape(4 * GROUP, LANES)
        asking = by_head(query[pair, 2 * tile : 2 * tile + 2].reshape(128, LANES))
        grads = by_head(gout[pair, 2 * tile : 2 * tile + 2].reshape(128, LANES))
        outside = jnp.concatenate([bias[...], bias[...]], axis=1)
        scores = dot(seen_keys, asking, ((1,), (1,))) + outside
        top = jnp.max(scores, axis=0, keepdims=True)
        raised = jnp.exp2((scores - top) * exponent)
        weights = raised * (1.0 / jnp.sum(raised, axis=0, keepdims=True))
        dweights = dot(seen_values, grads, ((1,), (1,)))
        correction = jnp.sum(weights * dweights, axis=0, keepdims=True)
        dscores = (weights * (dweights - correction)).astype(BF16)
        dkey = dot(dscores, asking, ((1,), (0,))) * rate
        dvalue = dot(weights.astype(BF16), grads, ((1,), (0,)))
        dquery = dot(dscores, seen_keys, ((0,), (0,)))
        dquery = jnp.where(low, dquery[:128], dquery[128:]) * rate
        lanes = pl.ds(pl.multiple_of(pair * LANES, LANES), LANES)
        grad_queries[128 * tile : 128 * tile + 128, lanes] = dquery.astype(BF16)
        return dkey, dvalue

    def turn_pole(buffer, chunk, dims):
        @pl.when(at_north | at_south)
        def _():
            for inner in range(PER_CHUNK):
                pair = chunk * PER_CHUNK + inner
                both = jnp.concatenate(
                    [buffer[pair, 0, pole_group], buffer[pair, 1, pole_group]], axis=1
                )
                turned = dot(turn[...], both, dims).astype(BF16)
                buffer[pair, 0, pole_group] = turned[:, :LANES]
                buffer[pair, 1, pole_group] = turned[:, LANES:]

    def pass_on(chunk):
        for copy in side_ends(chunk, True):
            copy.wait_recv()
        send_corners(chunk, True)

    def pass_back(chunk):
        for group, inward, polar in ((0, 1, at_north), (5, 4, at_south)):
            @pl.when(jnp.logical_not(polar))
            def _():
                for copy in part_ends(chunk, False, group, (-1, 1)):
                    copy.wait_recv()
                pairs_here = span(chunk)
                own = back[pairs_here, :, inward, 64:96, :].astype(F32)
                more = landed[pairs_here, :, group, 64:96, :].astype(F32)
                back[pairs_here, :, inward, 64:96, :] = (own + more).astype(BF16)
        send_sideways(chunk, False)

    def relay_all(chunk, carry):
        relay(chunk)
        return carry

    lax.fori_loop(0, chunks, relay_all, 0)
    pass_on(0)

    def work(chunk, carry):
        for inner in range(PER_CHUNK):
            for copy in loads(chunk * PER_CHUNK + inner, 1):
                copy.wait()
        row_ends(chunk, True, lambda copy: copy.wait_recv())
        for group in (0, 5):
            for copy in part_ends(chunk, True, group, (-1, 1)):
                copy.wait_recv()
        turn_pole(ext, chunk, ((1,), (0,)))
        for inner in range(PER_CHUNK):
            pair = chunk * PER_CHUNK + inner
            upper = attend(pair, 0)
            lower = attend(pair, 1)
            for kind in range(2):
                whole = jnp.concatenate(
                    [
                        upper[kind][: 2 * GROUP],
                        upper[kind][2 * GROUP :] + lower[kind][: 2 * GROUP],
                        lower[kind][2 * GROUP :],
                    ],
                    axis=0,
                ).reshape(6, GROUP, LANES)
                back[pair, kind] = whole.astype(BF16)
                total[pair, kind] = whole[1:5, 0:64].reshape(256, LANES)
            if inner == 0:
                @pl.when(chunk + 1 < chunks)
                def _():
                    pass_on(chunk + 1)

                @pl.when(chunk > 0)
                def _():
                    pass_back(chunk - 1)

        turn_pole(back, chunk, ((0,), (0,)))
        send_corners(chunk, False)
        send_rows(chunk, False)
        send_corners_across(chunk, False)
        return carry

    lax.fori_loop(0, chunks, work, 0)
    pass_back(chunks - 1)

    def finish(chunk, carry):
        for copy in side_ends(chunk, False):
            copy.wait_recv()
        row_ends(chunk, False, lambda copy: copy.wait_recv())
        for group, polar in ((0, at_north), (5, at_south)):
            @pl.when(polar)
            def _():
                for copy in part_ends(chunk, False, group, (-1, 1)):
                    copy.wait_recv()
        for inner in range(PER_CHUNK):
            pair = chunk * PER_CHUNK + inner
            lanes = pl.ds(pl.multiple_of(pair * LANES, LANES), LANES)
            for kind, out in ((0, grad_keys), (1, grad_values)):
                sides = landed[pair, kind, :, 64:96, :].reshape(192, LANES)
                whole = total[pair, kind] + dot(place[...], sides, ((1,), (0,)))
                first = whole[:64] + landed[pair, kind, 0, 0:64, :].astype(F32)
                last = whole[192:] + landed[pair, kind, 5, 0:64, :].astype(F32)
                out[0:64, lanes] = first.astype(BF16)
                out[64:192, lanes] = whole[64:192].astype(BF16)
                out[192:256, lanes] = last.astype(BF16)
        return carry

    lax.fori_loop(0, chunks, finish, 0)

    def drain(chunk, carry):
        for first in (True, False):
            for copy in side_ends(chunk, first):
                copy.wait_send()
            row_ends(chunk, first, lambda copy: copy.wait_send())
            for group in (0, 5):
                for copy in part_ends(chunk, first, group, (-1, 1)):
                    copy.wait_send()

        @pl.when(relays)
        def _():
            here = hop.at[span(chunk)]
            remote(
                here, here, hop_send_sem.at[chunk], hop_recv_sem.at[chunk], (pole_row, lon)
            ).wait_send()

        return carry

    lax.fori_loop(0, chunks, drain, 0)


def on_device(lat_count, lon_count, queries, keys, values, grad_out, fold_cols):
    height, breadth, features = queries.shape
    pairs = features // LANES
    chunks = pairs // PER_CHUNK
    cells = height * breadth
    inputs = [a.reshape(4, 64, features) for a in (queries, keys, values, grad_out)]
    window = (pairs, 2, 6, GROUP, LANES)
    out = jax.ShapeDtypeStruct((cells, features), BF16)
    results = pl.pallas_call(
        functools.partial(kernel, lat_count, lon_count, pairs),
        out_shape=(out, out, out),
        in_specs=[pl.BlockSpec(memory_space=pltpu.SMEM)]
        + [pl.BlockSpec(memory_space=pl.ANY)] * 4,
        out_specs=[pl.BlockSpec(memory_space=pltpu.VMEM)] * 3,
        scratch_shapes=[
            pltpu.VMEM(window, BF16),
            pltpu.VMEM((pairs, 2, 2, 4, 16, LANES), BF16),
            pltpu.VMEM(window, BF16),
            pltpu.VMEM(window, BF16),
            pltpu.VMEM((pairs, 4, 64, LANES), BF16),
            pltpu.VMEM((pairs, 4, 64, LANES), BF16),
            pltpu.VMEM((pairs, 2, cells, LANES), F32),
            pltpu.VMEM((4 * GROUP, 128), F32),
            pltpu.VMEM((128, 256), BF16),
            pltpu.VMEM((256, 192), BF16),
            pltpu.VMEM((GROUP, GROUP), BF16),
            pltpu.VMEM((pairs, 64, LANES), BF16),
            pltpu.SemaphoreType.DMA((pairs, 4)),
        ]
        + [pltpu.SemaphoreType.DMA((chunks, 9))] * 4
        + [pltpu.SemaphoreType.DMA((chunks,))] * 2,
        compiler_params=pltpu.CompilerParams(
            collective_id=0, has_side_effects=True, vmem_limit_bytes=60 << 20
        ),
        cost_estimate=pl.CostEstimate(
            flops=2_000_000_000, bytes_accessed=4_000_000, transcendentals=1_600_000
        ),
    )(fold_cols, *inputs)
    return tuple(r.reshape(height, breadth, features) for r in results)


def solution(mesh):
    block = P("lat", "lon", None)
    return jax.shard_map(
        functools.partial(on_device, mesh.shape["lat"], mesh.shape["lon"]),
        mesh=mesh,
        in_specs=(block, block, block, block, P()),
        out_specs=(block, block, block),
        check_vma=False,
    )
```
